128 devices in a mesh: tm: 4 (over y), space: 32 (over z, x, core).
Axes of the slice: x: 4, y: 4, z: 4, core: 2. Of those that a mesh axis runs over, the one named last changes fastest.
Arguments:
- record: bfloat16 [128, 3, 512, 1024], P('tm', None, 'space'), may hold values from -120 to 120, as said below
- last_slab: bfloat16 [32, 3, 512, 1024], P(None, None, 'space'), may hold values from -120 to 120, as said below
Outputs:
- density: float32 [32, 512, 1024], P('space', None, 'tm')
- top_two: float32 [32, 2], P('space')
The draws below stay inside these ranges and needn't reach their ends.
Inputs may be any that keep to these rules, and one draw needn't show every extreme that they name: `record`: three stress components, snapshots of a statistically varying flow. `last_slab`: the 32 snapshots right after record, of the same flow.
All inputs are finite; a program needn't handle non-finite values.
Results may differ from the reference program's by a relative error of at most 0.0003.
Values may be sent and summed in bfloat16 or wider, within the bound.
A program may use at most 256 MiB of HBM per device.

```python
import jax
import jax.numpy as jnp
from jax import lax

GY = 1024
BLOCK = 64
SWEEPS = 8
HOP = 32
F = 32
GX = 512
SNAP = 128
N_TM = 4
N_SPACE = 32


def scale_fields(key):
    cell_draw = jax.random.uniform(jax.random.fold_in(key, 11), (3, GX, GY), jnp.float32)
    time_draw = jax.random.uniform(jax.random.fold_in(key, 12), (SNAP + HOP, GX), jnp.float32)
    return (cell_draw, time_draw)


def shaped(key, first_id, num_rows, spread, noise_field):
    cell_draw, time_draw = scale_fields(key)
    cell_scale = jnp.exp(spread * (2.0 * cell_draw - 1.0))
    time_scale = jnp.exp(0.7 * (2.0 * time_draw[first_id:first_id + num_rows] - 1.0))
    ramp_rows = 1.0 + 2.0 * jnp.arange(GX).astype(jnp.float32) / max(GX - 1, 1)
    row_factor = time_scale * ramp_rows[None, :]
    return noise_field * cell_scale[None] * row_factor[:, None, :, None]


def draw_record(key, part):
    own_key = jax.random.fold_in(key, 1)
    noise_field = jnp.clip(jax.random.normal(own_key, (SNAP, 3, GX, GY), jnp.float32), -4.0, 4.0)
    values = shaped(key, 0, SNAP, 1.15, noise_field)
    return values.astype(jnp.bfloat16)


def draw_last_slab(key, part):
    own_key = jax.random.fold_in(key, 2)
    noise_field = jnp.clip(jax.random.normal(own_key, (HOP, 3, GX, GY), jnp.float32), -4.0, 4.0)
    values = shaped(key, SNAP, HOP, 1.15, noise_field)
    return values.astype(jnp.bfloat16)


def setup_inputs(seed: int = 0) -> dict:
    seeds = jax.random.split(jax.random.key(seed), 3)
    record = draw_record(jax.random.fold_in(seeds[2], 71), 0)
    last_slab = draw_last_slab(jax.random.fold_in(seeds[2], 71), 0)
    return {"record": record, "last_slab": last_slab}


def dft_table(length):
    half_len = length // 2
    sample_ids = jnp.arange(length, dtype=jnp.int32)
    phase_ids = jnp.arange(half_len, dtype=jnp.int32)[:, None] * sample_ids[None, :] % length
    angles = 2.0 * jnp.pi / length * phase_ids.astype(jnp.float32)
    taper_win = jnp.sqrt(8.0 / 3.0) * jnp.sin(jnp.pi * sample_ids.astype(jnp.float32) / length) ** 2 / jnp.sqrt(float(length))
    return jnp.concatenate([taper_win * jnp.cos(angles), -taper_win * jnp.sin(angles)], 0)

def spectra(block_data):
    length = block_data.shape[0]
    flat_data = block_data.astype(jnp.float32).reshape(length, -1)
    product = jnp.dot(dft_table(length), flat_data, precision=lax.Precision.HIGHEST)
    return product.reshape((2, length // 2) + block_data.shape[1:])

def gram_of(spectrum):
    block_count = spectrum.shape[0]
    flat_spec = spectrum.reshape(block_count, 2, spectrum.shape[2], -1)
    gram = jnp.einsum('brfk,csfk->frbsc', flat_spec, flat_spec, precision=lax.Precision.HIGHEST)
    return gram.reshape(spectrum.shape[2], 2 * block_count, 2 * block_count)

def complex_form(gram, cell_count):
    block_count = gram.shape[1] // 2
    real_part = gram[:, :block_count, :block_count] + gram[:, block_count:, block_count:]
    imag_part = gram[:, :block_count, block_count:] - gram[:, block_count:, :block_count]
    upper = jnp.concatenate([real_part, -imag_part], 2)
    lower = jnp.concatenate([imag_part, real_part], 2)
    return jnp.concatenate([upper, lower], 1) / cell_count

def jacobi(matrix):
    order = matrix.shape[0]
    vectors = jnp.broadcast_to(jnp.eye(order, dtype=matrix.dtype)[:, :, None], matrix.shape)
    for sweep in range(SWEEPS):
        for row_p in range(order - 1):
            for row_q in range(row_p + 1, order):
                diag_p = matrix[row_p, row_p]
                diag_q = matrix[row_q, row_q]
                offdiag = matrix[row_p, row_q]
                diff_pq = diag_q - diag_p
                sign_pq = jnp.where(diff_pq >= 0.0, 1.0, -1.0)
                denominator = jnp.abs(diff_pq) + jnp.sqrt(diff_pq * diff_pq + 4.0 * offdiag * offdiag)
                safe_denom = jnp.where(denominator > 0.0, denominator, 1.0)
                tangent = jnp.where(denominator > 0.0, 2.0 * offdiag * sign_pq / safe_denom, 0.0)
                cosine = 1.0 / jnp.sqrt(1.0 + tangent * tangent)
                sine = tangent * cosine
                column_p = matrix[:, row_p]
                column_q = matrix[:, row_q]
                matrix = matrix.at[:, row_p].set(cosine * column_p - sine * column_q)
                matrix = matrix.at[:, row_q].set(sine * column_p + cosine * column_q)
                line_p = matrix[row_p]
                line_q = matrix[row_q]
                matrix = matrix.at[row_p].set(cosine * line_p - sine * line_q)
                matrix = matrix.at[row_q].set(sine * line_p + cosine * line_q)
                vec_p = vectors[:, row_p]
                vec_q = vectors[:, row_q]
                vectors = vectors.at[:, row_p].set(cosine * vec_p - sine * vec_q)
                vectors = vectors.at[:, row_q].set(sine * vec_p + cosine * vec_q)
    eigvals = jnp.diagonal(matrix, 0, 0, 1).T
    return (eigvals, vectors)

def mode_weights(real_form):
    eigvals, vectors = jacobi(jnp.transpose(real_form, (1, 2, 0)))
    ordered = -jnp.sort(-eigvals, axis=0)
    leading = ordered[0]
    third_val = ordered[4]
    lifted = jnp.maximum(eigvals - third_val, 0.0)
    mode_matrix = jnp.einsum('ikf,kf,jkf->fij', vectors, lifted, vectors, precision=lax.Precision.HIGHEST)
    mode_matrix = mode_matrix / ((leading + 1e-06) ** 2)[:, None, None]
    return (mode_matrix, jnp.stack([ordered[0], ordered[2]], 1))

def density_of(spectrum, mode_matrix):
    block_count = spectrum.shape[0]
    freq_count = spectrum.shape[2]
    flat_spec = spectrum.reshape(block_count, 2, freq_count, -1)
    mode_split = mode_matrix.reshape(freq_count, 2, block_count, 2, block_count)
    applied = jnp.einsum('frbsc,csfk->brfk', mode_split, flat_spec, precision=lax.Precision.HIGHEST)
    energy = lax.optimization_barrier(jnp.sum(flat_spec * applied, axis=(0, 1)))
    return lax.optimization_barrier(jnp.sum(energy.reshape((freq_count,) + spectrum.shape[3:]), axis=1))

def band_spectra(series, first_row, row_count):
    band_rows = lax.dynamic_slice_in_dim(series, first_row, row_count, 2)
    return jnp.stack([spectra(band_rows[HOP * block_id:HOP * block_id + BLOCK]) for block_id in range(N_TM)], 0)

def reference(record, last_slab):
    series = jnp.concatenate([record, last_slab], 0)
    row_count = GX // N_SPACE
    cell_count = 3.0 * GX * GY

    def add_gram(gram_sum, band_index):
        spectrum = band_spectra(series, band_index * row_count, row_count)
        return (gram_sum + gram_of(spectrum), None)
    start_gram = jnp.zeros((F, 2 * N_TM, 2 * N_TM), jnp.float32)
    gram_sum, unused = lax.scan(add_gram, start_gram, jnp.arange(N_SPACE, dtype=jnp.int32))
    mode_matrix, top_two = mode_weights(complex_form(gram_sum, cell_count))

    def band_density(band_index):
        return density_of(band_spectra(series, band_index * row_count, row_count), mode_matrix)
    pieces = lax.map(band_density, jnp.arange(N_SPACE, dtype=jnp.int32))
    density = jnp.transpose(pieces, (1, 0, 2, 3)).reshape(F, GX, GY)
    return (density, top_two)
```

```python
import functools

import jax
import jax.numpy as jnp
import ml_dtypes
import numpy as np
from jax import lax
from jax.experimental import pallas as pl
from jax.experimental.pallas import tpu as pltpu
from jax.sharding import PartitionSpec as P

SWEEPS = 6
PARTS = 3
MESH = pl.DeviceIdType.MESH
F32 = jnp.float32
BF16 = jnp.bfloat16
PAIRS = [(b, c) for b in range(4) for c in range(b + 1, 4)]
ROUNDS = [((0, 1), (2, 3)), ((0, 2), (1, 3)), ((0, 3), (1, 2))]


def dft_rows():
    t = np.arange(64)
    taper = np.sqrt(8.0 / 3.0) * np.sin(np.pi * t / 64.0) ** 2 / 8.0
    angle = 2.0 * np.pi / 64.0 * ((np.arange(32)[:, None] * t[None, :]) % 64)
    rows = np.zeros((2, 4, 32, 160))
    for b in range(4):
        rows[0, b, :, 32 * b : 32 * b + 64] = taper * np.cos(angle)
        rows[1, b, :, 32 * b : 32 * b + 64] = -taper * np.sin(angle)
    return rows.reshape(256, 160)


def split_rows(rows, parts):
    left, out = rows.astype(np.float64), []
    for _ in range(parts):
        part = left.astype(ml_dtypes.bfloat16)
        out.append(part)
        left = left - part.astype(np.float64)
    return np.concatenate(out, 0)


def peers_along(axes, me):
    sizes = {"y": 4, "z": 4, "x": 4, "c": 2}
    out = []
    offsets = [{}]
    for a in axes:
        offsets = [dict(o, **{a: d}) for o in offsets for d in range(sizes[a])]
    for o in offsets:
        if any(o.values()):
            at = {a: (me[a] ^ o[a]) if o.get(a) else me[a] for a in me}
            out.append((at["y"], at["z"] * 8 + at["x"] * 2 + at["c"]))
    return out


def place(axes, me):
    sizes = {"y": 4, "z": 4, "x": 4, "c": 2}
    index = 0
    for a in axes:
        index = index * sizes[a] + me[a]
    return index


GROUPS = ("zxc", "y")


def eigen_modes(diag, off):
    one, zero = jnp.ones_like(diag[0]), jnp.zeros_like(diag[0])
    vec_re = [[one if i == k else zero for k in range(4)] for i in range(4)]
    vec_im = [[zero for k in range(4)] for i in range(4)]

    def sweep(_, state):
        diag, off_re, off_im, vec_re, vec_im = state
        diag = list(diag)
        mat = {pq: (off_re[i], off_im[i]) for i, pq in enumerate(PAIRS)}
        vec_re, vec_im = [list(r) for r in vec_re], [list(r) for r in vec_im]

        def get(i, k):
            if i < k:
                return mat[(i, k)]
            re, im = mat[(k, i)]
            return re, -im

        def put(i, k, re, im):
            if i < k:
                mat[(i, k)] = (re, im)
            else:
                mat[(k, i)] = (re, -im)

        for pivots in ROUNDS:
            turns = []
            for p, q in pivots:
                g_re, g_im = mat[(p, q)]
                diff = diag[q] - diag[p]
                size = g_re * g_re + g_im * g_im
                denom = jnp.abs(diff) + jnp.sqrt(diff * diff + 4.0 * size)
                some = denom > 0.0
                scale = jnp.where(some, jnp.where(diff >= 0.0, 2.0, -2.0), 0.0) / jnp.where(some, denom, 1.0)
                t_re, t_im = scale * g_re, -scale * g_im
                cosine = lax.rsqrt(1.0 + (t_re * t_re + t_im * t_im))
                shift = scale * size
                turns.append((p, q, cosine, cosine * t_re, cosine * t_im, shift))
            for p, q, cosine, s_re, s_im, shift in turns:
                diag[p], diag[q] = diag[p] - shift, diag[q] + shift
                mat[(p, q)] = (zero, zero)

                def rotate(col_p, col_q):
                    (pr, pi), (qr, qi) = col_p, col_q
                    new_p = (
                        cosine * pr - (s_re * qr - s_im * qi),
                        cosine * pi - (s_re * qi + s_im * qr),
                    )
                    new_q = (
                        cosine * qr + (s_re * pr + s_im * pi),
                        cosine * qi + (s_re * pi - s_im * pr),
                    )
                    return new_p, new_q

                for i in range(4):
                    if i not in (p, q):
                        new_p, new_q = rotate(get(i, p), get(i, q))
                        put(i, p, *new_p)
                        put(i, q, *new_q)
                    new_p, new_q = rotate((vec_re[i][p], vec_im[i][p]), (vec_re[i][q], vec_im[i][q]))
                    vec_re[i][p], vec_im[i][p] = new_p
                    vec_re[i][q], vec_im[i][q] = new_q
        off_re = [mat[pq][0] for pq in PAIRS]
        off_im = [mat[pq][1] for pq in PAIRS]
        return diag, off_re, off_im, vec_re, vec_im

    state = (list(diag), [off[pq][0] for pq in PAIRS], [off[pq][1] for pq in PAIRS], vec_re, vec_im)
    diag, _, _, vec_re, vec_im = lax.fori_loop(0, SWEEPS, sweep, state)
    return diag, vec_re, vec_im


def mode_terms(total, cells):
    sums = [total[k // 4 : k // 4 + 1, 32 * (k % 4) : 32 * (k % 4) + 32] / cells for k in range(16)]
    off = {pq: (sums[4 + i], sums[10 + i]) for i, pq in enumerate(PAIRS)}
    diag, vec_re, vec_im = eigen_modes(sums[:4], off)
    hi0, lo0 = jnp.maximum(diag[0], diag[1]), jnp.minimum(diag[0], diag[1])
    hi1, lo1 = jnp.maximum(diag[2], diag[3]), jnp.minimum(diag[2], diag[3])
    first = jnp.maximum(hi0, hi1)
    mid0, mid1 = jnp.minimum(hi0, hi1), jnp.maximum(lo0, lo1)
    second, third = jnp.maximum(mid0, mid1), jnp.minimum(mid0, mid1)
    norm = (first + 1e-06) * (first + 1e-06)
    lift = [jnp.maximum(d - third, 0.0) / norm for d in diag]
    terms = []
    for b in range(4):
        terms.append(sum(lift[k] * (vec_re[b][k] * vec_re[b][k] + vec_im[b][k] * vec_im[b][k]) for k in range(4)))
    for b, c in PAIRS:
        terms.append(2.0 * sum(lift[k] * (vec_re[b][k] * vec_re[c][k] + vec_im[b][k] * vec_im[c][k]) for k in range(4)))
    for b, c in PAIRS:
        terms.append(-2.0 * sum(lift[k] * (vec_im[b][k] * vec_re[c][k] - vec_re[b][k] * vec_im[c][k]) for k in range(4)))
    return terms, first, second


def kernel(
    cells, record, last, rows, out, top,
    slabs, wide, series, spec, prods, sums, turned, dens, part0, part1,
    send, recv, own, red_send, red_recv, out_send, out_recv, out_own,
):
    tm, space = lax.axis_index("tm"), lax.axis_index("space")
    me = {"y": tm, "z": space >> 3, "x": (space >> 1) & 3, "c": space & 1}
    parts = (part0, part1)

    barrier = pltpu.get_barrier_semaphore()
    ring = peers_along("y", me)
    plane = peers_along("zxc", me)
    for peer in ring + plane:
        pl.semaphore_signal(barrier, inc=1, device_id=peer, device_id_type=MESH)
    pl.semaphore_wait(barrier, len(ring) + len(plane))

    def quarter(ref, piece, to):
        half, comp = piece // 3, piece % 3
        return ref.at[:, comp, :, pl.ds(pl.multiple_of(to * 256 + half * 128, 128), 128)]

    def slab_copy(piece, d):
        to = tm ^ d
        return pltpu.make_async_remote_copy(
            src_ref=quarter(record, piece, to),
            dst_ref=slabs.at[tm, piece],
            send_sem=send.at[d - 1, piece],
            recv_sem=recv.at[d - 1, piece],
            device_id=(to, space),
            device_id_type=MESH,
        )

    def own_copy(piece, which):
        ref, slot = ((record, tm), (last, 4))[which]
        return pltpu.make_async_copy(quarter(ref, piece, tm), slabs.at[slot, piece], own.at[which, piece])

    for piece in range(6):
        for d in (2, 1, 3):
            slab_copy(piece, d).start()
    for piece in range(6):
        for which in range(2):
            own_copy(piece, which).start()

    zero = jnp.zeros((8, 128), F32)

    def clear(i, _):
        for half in range(2):
            for k in range(16):
                for g in range(4):
                    prods[half, i, k, 8 * g : 8 * g + 8, :] = zero
        return 0

    lax.fori_loop(0, 16, clear, 0)
    sums[...] = jnp.zeros_like(sums)

    def piece_step(piece, _):
        half = piece // 3
        for which in range(2):
            own_copy(piece, which).wait()
        for d in (1, 2, 3):
            slab_copy(piece, d).wait_recv()

        def lay_out(slab, _):
            wide[...] = slabs[slab, piece].astype(F32).reshape(512, 128)
            for n in range(8):
                for i in range(2):
                    lines = wide[pl.ds(2 * n + i, 32, stride=16), :].astype(BF16)
                    series[n, pl.ds(pl.multiple_of(slab * 32, 32), 32), 128 * i : 128 * i + 128] = lines
            return 0

        lax.fori_loop(0, 5, lay_out, 0)

        def transform(n, _):
            full = jnp.dot(rows[...], series[n], preferred_element_type=F32)
            spec[n] = sum(full[256 * i : 256 * i + 256] for i in range(1, PARTS)) + full[:256]
            return 0

        lax.fori_loop(0, 8, transform, 0)

        for g in range(4):

            def multiply(n, acc):
                acc = list(acc)
                for i in range(2):
                    x = [spec[n, 32 * m + 8 * g : 32 * m + 8 * g + 8, 128 * i : 128 * i + 128] for m in range(8)]
                    a, b = x[:4], x[4:]
                    terms = [a[u] * a[u] + b[u] * b[u] for u in range(4)]
                    terms += [a[u] * a[v] + b[u] * b[v] for u, v in PAIRS]
                    terms += [a[u] * b[v] - b[u] * a[v] for u, v in PAIRS]
                    for k in range(16):
                        prods[half, 2 * n + i, k, 8 * g : 8 * g + 8, :] += terms[k]
                        acc[k] = acc[k] + terms[k]
                return tuple(acc)

            acc = lax.fori_loop(0, 8, multiply, (zero,) * 16)
            for k in range(16):
                sums[32 * k + 8 * g : 32 * k + 8 * g + 8, :] += acc[k]
        return 0

    lax.fori_loop(0, 6, piece_step, 0)

    total = jnp.concatenate(
        [jnp.sum(jnp.transpose(sums[128 * i : 128 * i + 128, :]), axis=0, keepdims=True) for i in range(4)], 0
    )

    waits = []
    for stage, (axes, buf) in enumerate(zip(GROUPS, parts)):
        mine = place(axes, me)
        buf[mine] = total
        copies = []
        for d, peer in enumerate(peers_along(axes, me)):
            copy = pltpu.make_async_remote_copy(
                src_ref=buf.at[mine],
                dst_ref=buf.at[mine],
                send_sem=red_send.at[stage, d],
                recv_sem=red_recv.at[stage, d],
                device_id=peer,
                device_id_type=MESH,
            )
            copy.start()
            copies.append(copy)
        for copy in copies:
            copy.wait_recv()
        total = jnp.sum(buf[...], axis=0)
        waits += copies

    terms, first, second = mode_terms(total, cells)
    here = lax.broadcasted_iota(jnp.int32, (1, 32), 1) == space
    pick = [jnp.sum(jnp.where(here, v, 0.0), axis=1, keepdims=True) for v in (first, second)]
    top[...] = jnp.concatenate(pick, 1)

    for k in range(16):
        turned[k : k + 1, 0:32] = terms[k]
    columns = jnp.transpose(turned[...])

    for g in range(4):
        weight = [jnp.broadcast_to(columns[8 * g : 8 * g + 8, k : k + 1], (8, 128)) for k in range(16)]

        def collect(r, _):
            for half in range(2):
                value = weight[0] * prods[half, r, 0, 8 * g : 8 * g + 8, :]
                for k in range(1, 16):
                    value += weight[k] * prods[half, r, k, 8 * g : 8 * g + 8, :]
                dens[pl.ds(256 * g + 16 * (r // 8) + 8 * half + r % 8, 8, stride=32), :] = value
            return 0

        lax.fori_loop(0, 16, collect, 0)

    def tiles_of(index):
        return pl.ds(pl.multiple_of(index * 32, 32), 32)

    kept = pltpu.make_async_copy(dens.at[tiles_of(space)], out.at[tiles_of(space)], out_own)
    kept.start()
    copies = []
    for d, peer in enumerate(plane):
        copy = pltpu.make_async_remote_copy(
            src_ref=dens.at[tiles_of(peer[1])],
            dst_ref=out.at[tiles_of(space)],
            send_sem=out_send.at[d],
            recv_sem=out_recv.at[d],
            device_id=peer,
            device_id_type=MESH,
        )
        copy.start()
        copies.append(copy)
    for copy in waits:
        copy.wait_send()
    for piece in range(6):
        for d in (1, 2, 3):
            slab_copy(piece, d).wait_send()
    kept.wait()
    for copy in copies:
        copy.wait()


def body(record, last_slab):
    cells = float(record.shape[1] * record.shape[2] * lax.axis_size("space") * record.shape[3])
    rows = jnp.asarray(split_rows(dft_rows(), PARTS))
    dma = pltpu.SemaphoreType.DMA
    tiles, top = pl.pallas_call(
        functools.partial(kernel, cells),
        out_shape=(jax.ShapeDtypeStruct((1024, 128), F32), jax.ShapeDtypeStruct((1, 2), F32)),
        in_specs=[
            pl.BlockSpec(memory_space=pl.ANY),
            pl.BlockSpec(memory_space=pl.ANY),
            pl.BlockSpec(memory_space=pltpu.VMEM),
        ],
        out_specs=(pl.BlockSpec(memory_space=pl.ANY), pl.BlockSpec(memory_space=pltpu.VMEM)),
        scratch_shapes=[
            pltpu.VMEM((5, 6, 32, 16, 128), BF16),
            pltpu.VMEM((512, 128), F32),
            pltpu.VMEM((8, 160, 256), BF16),
            pltpu.VMEM((8, 256, 256), F32),
            pltpu.VMEM((2, 16, 16, 32, 128), F32),
            pltpu.VMEM((512, 128), F32),
            pltpu.VMEM((128, 128), F32),
            pltpu.VMEM((1024, 128), F32),
            pltpu.VMEM((32, 4, 128), F32),
            pltpu.VMEM((4, 4, 128), F32),
            dma((3, 6)),
            dma((3, 6)),
            dma((2, 6)),
            dma((2, 31)),
            dma((2, 31)),
            dma((31,)),
            dma((31,)),
            dma(()),
        ],
        compiler_params=pltpu.CompilerParams(
            collective_id=0, has_side_effects=True, vmem_limit_bytes=48 << 20
        ),
        name="modes",
    )(record, last_slab, rows)
    density = tiles.reshape(64, 2, 8, 128).transpose(0, 2, 1, 3).reshape(1, 512, 256)
    return density, top


def solution(mesh):
    return jax.shard_map(
        body,
        mesh=mesh,
        in_specs=(P("tm", None, "space", None), P(None, None, "space", None)),
        out_specs=(P("space", None, "tm"), P("space", None)),
        check_vma=False,
    )
```

```python
import functools

import jax
import jax.numpy as jnp
import numpy as np
from jax import lax
from jax.experimental import pallas as pl
from jax.experimental.pallas import tpu as pltpu
from jax.sharding import PartitionSpec as P

SWEEPS = 5
MESH = pl.DeviceIdType.MESH
F32 = jnp.float32
BF16 = jnp.bfloat16
PAIRS = [(b, c) for b in range(4) for c in range(b + 1, 4)]
ROUNDS = [((0, 1), (2, 3)), ((0, 2), (1, 3)), ((0, 3), (1, 2))]


def dft_rows():
    row = lax.broadcasted_iota(jnp.int32, (256, 160), 0)
    t = lax.broadcasted_iota(jnp.int32, (256, 160), 1) - 32 * ((row >> 5) & 3)
    turn = 2.0 * np.pi / 64.0
    taper = np.sqrt(8.0 / 3.0) / 16.0 * (1.0 - jnp.cos(turn * t.astype(F32)))
    phase = ((row & 31) * t + jnp.where(row >= 128, 16, 0) + 32) & 63
    wave = jnp.cos(turn * (phase - 32).astype(F32))
    return jnp.where((t >= 0) & (t < 64), taper * wave, 0.0)


def peers_along(axes, me):
    sizes = {"y": 4, "z": 4, "x": 4, "c": 2}
    out = []
    offsets = [{}]
    for a in axes:
        offsets = [dict(o, **{a: d}) for o in offsets for d in range(sizes[a])]
    for o in offsets:
        if any(o.values()):
            at = {a: (me[a] ^ o[a]) if o.get(a) else me[a] for a in me}
            out.append((at["y"], at["z"] * 8 + at["x"] * 2 + at["c"]))
    return out


def place(axes, me):
    sizes = {"y": 4, "z": 4, "x": 4, "c": 2}
    index = 0
    for a in axes:
        index = index * sizes[a] + me[a]
    return index


GROUPS = ("zxc", "y")


def eigen_modes(diag, off):
    zero = jnp.zeros_like(diag[0])
    copy = lax.broadcasted_iota(jnp.int32, zero.shape, 1) >> 5
    vecs = [(jnp.where(copy == k, 1.0, 0.0), zero) for k in range(4)]

    def sweep(_, state):
        diag, mat, vecs = list(state[0]), dict(zip(PAIRS, state[1])), list(state[2])

        def get(i, k):
            if i < k:
                return mat[(i, k)]
            re, im = mat[(k, i)]
            return re, -im

        def put(i, k, entry):
            mat[(min(i, k), max(i, k))] = entry if i < k else (entry[0], -entry[1])

        for pivots in ROUNDS:
            turns = []
            for p, q in pivots:
                g_re, g_im = mat[(p, q)]
                diff = diag[q] - diag[p]
                size = g_re * g_re + g_im * g_im
                gap = diff * diff + 4.0 * size
                some = gap > 0.0
                inverse = lax.rsqrt(jnp.where(some, gap, 1.0))
                square = jnp.where(some, 0.5 + 0.5 * jnp.abs(diff) * inverse, 1.0)
                secant = lax.rsqrt(square)
                signed = jnp.where(diff >= 0.0, inverse, -inverse)
                factor = signed * secant
                turns.append((p, q, square * secant, factor * g_re, -factor * g_im, size * factor * secant))
            for p, q, cosine, s_re, s_im, shift in turns:
                diag[p], diag[q] = diag[p] - shift, diag[q] + shift
                mat[(p, q)] = (zero, zero)

                def rotate(col_p, col_q):
                    (pr, pi), (qr, qi) = col_p, col_q
                    new_p = (cosine * pr - (s_re * qr - s_im * qi), cosine * pi - (s_re * qi + s_im * qr))
                    new_q = (cosine * qr + (s_re * pr + s_im * pi), cosine * qi + (s_re * pi - s_im * pr))
                    return new_p, new_q

                for i in range(4):
                    if i not in (p, q):
                        new_p, new_q = rotate(get(i, p), get(i, q))
                        put(i, p, new_p)
                        put(i, q, new_q)
                vecs[p], vecs[q] = rotate(vecs[p], vecs[q])
        return diag, [mat[pq] for pq in PAIRS], vecs

    state = (list(diag), [off[pq] for pq in PAIRS], vecs)
    diag, _, vecs = lax.fori_loop(0, SWEEPS, sweep, state)
    return diag, vecs


def mode_terms(total, cells):
    def spread(k):
        part = total[k // 4 : k // 4 + 1, 32 * (k % 4) : 32 * (k % 4) + 32] * (1.0 / cells)
        return jnp.concatenate([part] * 4, 1)

    sums = [spread(k) for k in range(16)]
    off = {pq: (sums[4 + i], sums[10 + i]) for i, pq in enumerate(PAIRS)}
    diag, vecs = eigen_modes(sums[:4], off)
    hi0, lo0 = jnp.maximum(diag[0], diag[1]), jnp.minimum(diag[0], diag[1])
    hi1, lo1 = jnp.maximum(diag[2], diag[3]), jnp.minimum(diag[2], diag[3])
    first = jnp.maximum(hi0, hi1)
    mid0, mid1 = jnp.minimum(hi0, hi1), jnp.maximum(lo0, lo1)
    second, third = jnp.maximum(mid0, mid1), jnp.minimum(mid0, mid1)
    norm = (first + 1e-06) * (first + 1e-06)
    lift = [jnp.maximum(d - third, 0.0) / norm for d in diag]
    mode = []
    for d in range(3):
        re, im = 0.0, 0.0
        for k in range(4):
            ar, ai = vecs[k]
            br, bi = (pltpu.roll(v, 128 - 32 * d, 1) if d else v for v in vecs[k])
            re = re + lift[k] * (ar * br + ai * bi)
            im = im + lift[k] * (ai * br - ar * bi)
        mode.append((re, im))
    terms = [mode[0][0][:, 32 * b : 32 * b + 32] for b in range(4)]
    for part in range(2):
        for b, c in PAIRS:
            d = c - b
            at, sign = (b, 1.0) if d < 3 else (3, (1.0, -1.0)[part])
            entry = mode[d if d < 3 else 1][part][:, 32 * at : 32 * at + 32]
            terms.append((2.0, -2.0)[part] * sign * entry)
    return terms, first[:, 0:32], second[:, 0:32]


def kernel(
    cells, record, last, out, top,
    slabs, split, wide, series, spec0, spec1, prods, sums, turned, weights, dens, part0, part1,
    send, recv, own, red_send, red_recv, out_send, out_recv, out_own,
):
    tm, space = lax.axis_index("tm"), lax.axis_index("space")
    me = {"y": tm, "z": space >> 3, "x": (space >> 1) & 3, "c": space & 1}
    parts = (part0, part1)

    barrier = pltpu.get_barrier_semaphore()
    ring = peers_along("y", me)
    plane = peers_along("zxc", me)
    for peer in ring + plane:
        pl.semaphore_signal(barrier, inc=1, device_id=peer, device_id_type=MESH)

    def quarter(ref, piece, to):
        half, comp = piece // 3, piece % 3
        return ref.at[:, comp, :, pl.ds(pl.multiple_of(to * 256 + half * 128, 128), 128)]

    def slab_copy(piece, d):
        to = tm ^ d
        return pltpu.make_async_remote_copy(
            src_ref=quarter(record, piece, to),
            dst_ref=slabs.at[tm, piece],
            send_sem=send.at[d - 1, piece],
            recv_sem=recv.at[d - 1, piece],
            device_id=(to, space),
            device_id_type=MESH,
        )

    def own_copy(piece, which):
        ref, slot = ((record, tm), (last, 4))[which]
        return pltpu.make_async_copy(quarter(ref, piece, tm), slabs.at[slot, piece], own.at[which, piece])

    for piece in range(6):
        for which in range(2):
            own_copy(piece, which).start()
    pl.semaphore_wait(barrier, len(ring) + len(plane))
    for piece in range(6):
        for d in (2, 1, 3):
            slab_copy(piece, d).start()

    sums[...] = jnp.zeros_like(sums)
    table = dft_rows()
    upper = table.astype(BF16)
    split[0:256, :] = upper
    split[256:512, :] = (table - upper.astype(F32)).astype(BF16)

    def multiply(half, comp, n, spec):
        for g in range(4):
            for i in range(2):
                x = [spec[32 * m + 8 * g : 32 * m + 8 * g + 8, 128 * i : 128 * i + 128] for m in range(8)]
                a, b = x[:4], x[4:]
                terms = [a[u] * a[u] + b[u] * b[u] for u in range(4)]
                terms += [a[u] * a[v] + b[u] * b[v] for u, v in PAIRS]
                terms += [a[u] * b[v] - b[u] * a[v] for u, v in PAIRS]
                for k in range(16):
                    if comp > 0:
                        terms[k] += prods[half, 2 * n + i, k, 8 * g : 8 * g + 8, :]
                    prods[half, 2 * n + i, k, 8 * g : 8 * g + 8, :] = terms[k]
                    if comp == 2:
                        sums[32 * k + 8 * g : 32 * k + 8 * g + 8, :] += terms[k]

    def transform(n, spec):
        full = jnp.dot(split[...], series[n], preferred_element_type=F32)
        spec[...] = full[256:512] + full[0:256]

    def half_step(half, _):
        for comp in range(3):
            piece = 3 * half + comp
            for which in range(2):
                own_copy(piece, which).wait()
            for d in (1, 2, 3):
                slab_copy(piece, d).wait_recv()

            def lay_out(slab, _, piece=piece):
                wide[...] = slabs[slab, piece].astype(F32).reshape(512, 128)
                for n in range(8):
                    for i in range(2):
                        lines = wide[pl.ds(2 * n + i, 32, stride=16), :].astype(BF16)
                        series[n, pl.ds(pl.multiple_of(slab * 32, 32), 32), 128 * i : 128 * i + 128] = lines
                return 0

            lax.fori_loop(0, 5, lay_out, 0)
            specs = (spec0, spec1)
            transform(0, spec0)
            for n in range(8):
                if n < 7:
                    transform(n + 1, specs[(n + 1) % 2])
                multiply(half, comp, n, specs[n % 2])
        return 0

    lax.fori_loop(0, 2, half_step, 0)

    total = jnp.concatenate(
        [jnp.sum(jnp.transpose(sums[128 * i : 128 * i + 128, :]), axis=0, keepdims=True) for i in range(4)], 0
    )

    waits = []
    for stage, (axes, buf) in enumerate(zip(GROUPS, parts)):
        mine = place(axes, me)
        buf[mine] = total
        copies = []
        for d, peer in enumerate(peers_along(axes, me)):
            copy = pltpu.make_async_remote_copy(
                src_ref=buf.at[mine],
                dst_ref=buf.at[mine],
                send_sem=red_send.at[stage, d],
                recv_sem=red_recv.at[stage, d],
                device_id=peer,
                device_id_type=MESH,
            )
            copy.start()
            copies.append(copy)
        for copy in copies:
            copy.wait_recv()
        total = jnp.sum(buf[...], axis=0)
        waits += copies

    terms, first, second = mode_terms(total, cells)
    here = lax.broadcasted_iota(jnp.int32, (1, 32), 1) == space
    pick = [jnp.sum(jnp.where(here, v, 0.0), axis=1, keepdims=True) for v in (first, second)]
    top[...] = jnp.concatenate(pick, 1)

    for k in range(16):
        turned[k : k + 1, 0:32] = terms[k]
    columns = jnp.transpose(turned[...])

    for g in range(4):
        for k in range(16):
            weights[g, k] = jnp.broadcast_to(columns[8 * g : 8 * g + 8, k : k + 1], (8, 128))

    def tiles_of(index):
        return pl.ds(pl.multiple_of(index * 32, 32), 32)

    kept = pltpu.make_async_copy(dens.at[tiles_of(space)], out.at[tiles_of(space)], out_own)
    copies = []
    for step in range(4):
        g = me["z"] ^ step
        band = pl.ds(pl.multiple_of(8 * g, 8), 8)
        weight = [weights[g, k] for k in range(16)]

        def collect(r, _, g=g, band=band, weight=weight):
            for half in range(2):
                parts = [weight[k] * prods[half, r, k, band, :] for k in range(16)]
                while len(parts) > 1:
                    parts = [parts[k] + parts[k + 1] for k in range(0, len(parts), 2)]
                dens[pl.ds(256 * g + 16 * (r // 8) + 8 * half + r % 8, 8, stride=32), :] = parts[0]
            return 0

        lax.fori_loop(0, 16, collect, 0, unroll=4)
        for i in range(8):
            if step == 0 and i == 0:
                kept.start()
                continue
            d = 8 * step + i
            peer = space ^ d
            copy = pltpu.make_async_remote_copy(
                src_ref=dens.at[tiles_of(peer)],
                dst_ref=out.at[tiles_of(space)],
                send_sem=out_send.at[d - 1],
                recv_sem=out_recv.at[d - 1],
                device_id=(tm, peer),
                device_id_type=MESH,
            )
            copy.start()
            copies.append(copy)
    for copy in waits:
        copy.wait_send()
    for piece in range(6):
        for d in (1, 2, 3):
            slab_copy(piece, d).wait_send()
    kept.wait()
    for copy in copies:
        copy.wait()


def body(record, last_slab):
    cells = float(record.shape[1] * record.shape[2] * lax.axis_size("space") * record.shape[3])
    dma = pltpu.SemaphoreType.DMA
    tiles, top = pl.pallas_call(
        functools.partial(kernel, cells),
        out_shape=(jax.ShapeDtypeStruct((1024, 128), F32), jax.ShapeDtypeStruct((1, 2), F32)),
        in_specs=[
            pl.BlockSpec(memory_space=pl.ANY),
            pl.BlockSpec(memory_space=pl.ANY),
        ],
        out_specs=(pl.BlockSpec(memory_space=pl.ANY), pl.BlockSpec(memory_space=pltpu.VMEM)),
        scratch_shapes=[
            pltpu.VMEM((5, 6, 32, 16, 128), BF16),
            pltpu.VMEM((512, 160), BF16),
            pltpu.VMEM((512, 128), F32),
            pltpu.VMEM((8, 160, 256), BF16),
            pltpu.VMEM((256, 256), F32),
            pltpu.VMEM((256, 256), F32),
            pltpu.VMEM((2, 16, 16, 32, 128), F32),
            pltpu.VMEM((512, 128), F32),
            pltpu.VMEM((128, 128), F32),
            pltpu.VMEM((4, 16, 8, 128), F32),
            pltpu.VMEM((1024, 128), F32),
            pltpu.VMEM((32, 4, 128), F32),
            pltpu.VMEM((4, 4, 128), F32),
            dma((3, 6)),
            dma((3, 6)),
            dma((2, 6)),
            dma((2, 31)),
            dma((2, 31)),
            dma((31,)),
            dma((31,)),
            dma(()),
        ],
        compiler_params=pltpu.CompilerParams(
            collective_id=0, has_side_effects=True, vmem_limit_bytes=52 << 20
        ),
        name="modes",
    )(record, last_slab)
    density = tiles.reshape(64, 2, 8, 128).transpose(0, 2, 1, 3).reshape(1, 512, 256)
    return density, top


def solution(mesh):
    return jax.shard_map(
        body,
        mesh=mesh,
        in_specs=(P("tm", None, "space", None), P(None, None, "space", None)),
        out_specs=(P("space", None, "tm"), P("space", None)),
        check_vma=False,
    )
```

```python
import functools
import math

import jax
import jax.numpy as jnp
import numpy as np
from jax import lax
from jax.experimental import pallas as pl
from jax.experimental.pallas import tpu as pltpu
from jax.sharding import PartitionSpec as P

SWEEPS = 5
MESH = pl.DeviceIdType.MESH
F32 = jnp.float32
BF16 = jnp.bfloat16
PAIRS = [(b, c) for b in range(4) for c in range(b + 1, 4)]
SIZES = {"y": 4, "z": 4, "x": 4, "c": 2}
ROUNDS = [((0, 1), (2, 3)), ((0, 2), (1, 3)), ((0, 3), (1, 2))]


def dft_rows():
    row = lax.broadcasted_iota(jnp.int32, (256, 160), 0)
    t = lax.broadcasted_iota(jnp.int32, (256, 160), 1) - 32 * ((row >> 5) & 3)
    turn = 2.0 * np.pi / 64.0
    taper = np.sqrt(8.0 / 3.0) / 16.0 * (1.0 - jnp.cos(turn * t.astype(F32)))
    phase = ((row & 31) * t + jnp.where(row >= 128, 16, 0) + 32) & 63
    wave = jnp.cos(turn * (phase - 32).astype(F32))
    return jnp.where((t >= 0) & (t < 64), taper * wave, 0.0)


def peers_along(axes, me):
    out = []
    offsets = [{}]
    for a in axes:
        offsets = [dict(o, **{a: d}) for o in offsets for d in range(SIZES[a])]
    for o in offsets:
        if any(o.values()):
            at = {a: (me[a] ^ o[a]) if o.get(a) else me[a] for a in me}
            out.append((at["y"], at["z"] * 8 + at["x"] * 2 + at["c"]))
    return out


def place(axes, me):
    index = 0
    for a in axes:
        index = index * SIZES[a] + me[a]
    return index


GROUPS = ("zxc", "y")


def eigen_modes(diag, off):
    zero = jnp.zeros_like(diag[0])
    copy = lax.broadcasted_iota(jnp.int32, zero.shape, 1) >> 5
    vecs = [(jnp.where(copy == k, 1.0, 0.0), zero) for k in range(4)]

    def sweep(_, state):
        diag, mat, vecs = list(state[0]), dict(zip(PAIRS, state[1])), list(state[2])

        def get(i, k):
            if i < k:
                return mat[(i, k)]
            re, im = mat[(k, i)]
            return re, -im

        def put(i, k, entry):
            mat[(min(i, k), max(i, k))] = entry if i < k else (entry[0], -entry[1])

        for pivots in ROUNDS:
            turns = []
            for p, q in pivots:
                g_re, g_im = mat[(p, q)]
                diff = diag[q] - diag[p]
                size = g_re * g_re + g_im * g_im
                gap = diff * diff + 4.0 * size
                some = gap > 0.0
                inverse = lax.rsqrt(jnp.where(some, gap, 1.0))
                square = jnp.where(some, 0.5 + 0.5 * jnp.abs(diff) * inverse, 1.0)
                secant = lax.rsqrt(square)
                signed = jnp.where(diff >= 0.0, inverse, -inverse)
                factor = signed * secant
                turns.append((p, q, square * secant, factor * g_re, -factor * g_im, size * factor * secant))
            for p, q, cosine, s_re, s_im, shift in turns:
                diag[p], diag[q] = diag[p] - shift, diag[q] + shift
                mat[(p, q)] = (zero, zero)

                def rotate(col_p, col_q):
                    (pr, pi), (qr, qi) = col_p, col_q
                    new_p = (cosine * pr - (s_re * qr - s_im * qi), cosine * pi - (s_re * qi + s_im * qr))
                    new_q = (cosine * qr + (s_re * pr + s_im * pi), cosine * qi + (s_re * pi - s_im * pr))
                    return new_p, new_q

                for i in range(4):
                    if i not in (p, q):
                        new_p, new_q = rotate(get(i, p), get(i, q))
                        put(i, p, new_p)
                        put(i, q, new_q)
                vecs[p], vecs[q] = rotate(vecs[p], vecs[q])
        return diag, [mat[pq] for pq in PAIRS], vecs

    state = (list(diag), [off[pq] for pq in PAIRS], vecs)
    diag, _, vecs = lax.fori_loop(0, SWEEPS, sweep, state)
    return diag, vecs


def mode_terms(total, cells):
    def spread(k):
        part = total[k // 4 : k // 4 + 1, 32 * (k % 4) : 32 * (k % 4) + 32] * (1.0 / cells)
        return jnp.concatenate([part] * 4, 1)

    sums = [spread(k) for k in range(16)]
    off = {pq: (sums[4 + i], sums[10 + i]) for i, pq in enumerate(PAIRS)}
    diag, vecs = eigen_modes(sums[:4], off)
    hi0, lo0 = jnp.maximum(diag[0], diag[1]), jnp.minimum(diag[0], diag[1])
    hi1, lo1 = jnp.maximum(diag[2], diag[3]), jnp.minimum(diag[2], diag[3])
    first = jnp.maximum(hi0, hi1)
    mid0, mid1 = jnp.minimum(hi0, hi1), jnp.maximum(lo0, lo1)
    second, third = jnp.maximum(mid0, mid1), jnp.minimum(mid0, mid1)
    norm = (first + 1e-06) * (first + 1e-06)
    lift = [jnp.maximum(d - third, 0.0) / norm for d in diag]
    mode = []
    for d in range(3):
        re, im = 0.0, 0.0
        for k in range(4):
            ar, ai = vecs[k]
            br, bi = (pltpu.roll(v, 128 - 32 * d, 1) if d else v for v in vecs[k])
            re = re + lift[k] * (ar * br + ai * bi)
            im = im + lift[k] * (ai * br - ar * bi)
        mode.append((re, im))
    terms = [mode[0][0][:, 32 * b : 32 * b + 32] for b in range(4)]
    for part in range(2):
        for b, c in PAIRS:
            d = c - b
            at, sign = (b, 1.0) if d < 3 else (3, (1.0, -1.0)[part])
            entry = mode[d if d < 3 else 1][part][:, 32 * at : 32 * at + 32]
            terms.append((2.0, -2.0)[part] * sign * entry)
    return terms, first[:, 0:32], second[:, 0:32]


def kernel(
    cells, record, last, out, top,
    slabs, split, wide, series, spec0, spec1, prods, sums, turned, weights, dens, *rest,
):
    tm, space = lax.axis_index("tm"), lax.axis_index("space")
    me = {"y": tm, "z": space >> 3, "x": (space >> 1) & 3, "c": space & 1}
    parts = rest[: len(GROUPS)]
    send, recv, red_send, red_recv, out_send, out_recv, meet = rest[len(GROUPS) :]

    near = [peer for axis in "cxzy" for peer in peers_along(axis, me)]

    def greet(semaphore):
        for peer in near:
            pl.semaphore_signal(semaphore, inc=1, device_id=peer, device_id_type=MESH)

    def landed(ref, semaphore):
        pltpu.make_async_copy(ref, ref, semaphore).wait()

    barrier = pltpu.get_barrier_semaphore()
    greet(barrier)

    def quarter(ref, piece, to):
        half, comp = piece // 3, piece % 3
        return ref.at[:, comp, :, pl.ds(pl.multiple_of(to * 256 + half * 128, 128), 128)]

    def slab_copy(piece, d):
        to = tm ^ d
        return pltpu.make_async_remote_copy(
            src_ref=quarter(record, piece, to),
            dst_ref=slabs.at[tm, piece],
            send_sem=send,
            recv_sem=recv.at[piece],
            device_id=(to, space),
            device_id_type=MESH,
        )

    def own_copy(piece, which):
        ref, slot = ((record, tm), (last, 4))[which]
        return pltpu.make_async_copy(quarter(ref, piece, tm), slabs.at[slot, piece], recv.at[piece])

    for piece in range(6):
        for which in range(2):
            own_copy(piece, which).start()
    pl.semaphore_wait(barrier, len(near))
    for piece in range(6):
        for d in (2, 1, 3):
            slab_copy(piece, d).start()
    for turn in range(3):
        greet(meet.at[turn])
        pl.semaphore_wait(meet.at[turn], len(near))

    sums[...] = jnp.zeros_like(sums)
    table = dft_rows()
    upper = table.astype(BF16)
    split[0:256, :] = upper
    split[256:512, :] = (table - upper.astype(F32)).astype(BF16)

    def multiply(half, comp, n, spec):
        for g in range(4):
            for i in range(2):
                x = [spec[32 * m + 8 * g : 32 * m + 8 * g + 8, 128 * i : 128 * i + 128] for m in range(8)]
                a, b = x[:4], x[4:]
                terms = [a[u] * a[u] + b[u] * b[u] for u in range(4)]
                terms += [a[u] * a[v] + b[u] * b[v] for u, v in PAIRS]
                terms += [a[u] * b[v] - b[u] * a[v] for u, v in PAIRS]
                for k in range(16):
                    if comp > 0:
                        terms[k] += prods[half, 2 * n + i, k, 8 * g : 8 * g + 8, :]
                    prods[half, 2 * n + i, k, 8 * g : 8 * g + 8, :] = terms[k]
                    if comp == 2:
                        sums[32 * k + 8 * g : 32 * k + 8 * g + 8, :] += terms[k]

    def transform(n, spec):
        full = jnp.dot(split[...], series[n], preferred_element_type=F32)
        spec[...] = full[256:512] + full[0:256]

    def half_step(half, _):
        for comp in range(3):
            piece = 3 * half + comp
            landed(slabs.at[:, piece], recv.at[piece])

            def lay_out(slab, _, piece=piece):
                wide[...] = slabs[slab, piece].astype(F32).reshape(512, 128)
                for n in range(8):
                    for i in range(2):
                        lines = wide[pl.ds(2 * n + i, 32, stride=16), :].astype(BF16)
                        series[n, pl.ds(pl.multiple_of(slab * 32, 32), 32), 128 * i : 128 * i + 128] = lines
                return 0

            lax.fori_loop(0, 5, lay_out, 0)
            specs = (spec0, spec1)
            transform(0, spec0)
            for n in range(8):
                if n < 7:
                    transform(n + 1, specs[(n + 1) % 2])
                multiply(half, comp, n, specs[n % 2])
        return 0

    lax.fori_loop(0, 2, half_step, 0)

    total = jnp.concatenate(
        [jnp.sum(jnp.transpose(sums[128 * i : 128 * i + 128, :]), axis=0, keepdims=True) for i in range(4)], 0
    )

    for stage, (axes, buf) in enumerate(zip(GROUPS, parts)):
        mine = place(axes, me)
        buf[mine] = total
        for peer in peers_along(axes, me):
            pltpu.make_async_remote_copy(
                src_ref=buf.at[mine],
                dst_ref=buf.at[mine],
                send_sem=red_send.at[stage],
                recv_sem=red_recv.at[stage],
                device_id=peer,
                device_id_type=MESH,
            ).start()
        landed(buf.at[pl.ds(0, buf.shape[0] - 1)], red_recv.at[stage])
        total = jnp.sum(buf[...], axis=0)

    terms, first, second = mode_terms(total, cells)
    here = lax.broadcasted_iota(jnp.int32, (1, 32), 1) == space
    pick = [jnp.sum(jnp.where(here, v, 0.0), axis=1, keepdims=True) for v in (first, second)]
    top[...] = jnp.concatenate(pick, 1)

    for k in range(16):
        turned[k : k + 1, 0:32] = terms[k]
    columns = jnp.transpose(turned[...])

    for g in range(4):
        for k in range(16):
            weights[g, k] = jnp.broadcast_to(columns[8 * g : 8 * g + 8, k : k + 1], (8, 128))

    def tiles_of(index):
        return pl.ds(pl.multiple_of(index * 32, 32), 32)

    kept = pltpu.make_async_copy(dens.at[tiles_of(space)], out.at[tiles_of(space)], out_recv)
    for step in range(4):
        g = me["z"] ^ step
        band = pl.ds(pl.multiple_of(8 * g, 8), 8)
        weight = [weights[g, k] for k in range(16)]

        def collect(r, _, g=g, band=band, weight=weight):
            for half in range(2):
                parts = [weight[k] * prods[half, r, k, band, :] for k in range(16)]
                while len(parts) > 1:
                    parts = [parts[k] + parts[k + 1] for k in range(0, len(parts), 2)]
                dens[pl.ds(256 * g + 16 * (r // 8) + 8 * half + r % 8, 8, stride=32), :] = parts[0]
            return 0

        lax.fori_loop(0, 16, collect, 0, unroll=4)
        for i in range(8):
            if step == 0 and i == 0:
                kept.start()
                continue
            d = 8 * step + i
            peer = space ^ d
            pltpu.make_async_remote_copy(
                src_ref=dens.at[tiles_of(peer)],
                dst_ref=out.at[tiles_of(space)],
                send_sem=out_send,
                recv_sem=out_recv,
                device_id=(tm, peer),
                device_id_type=MESH,
            ).start()
    for stage, buf in enumerate(parts):
        landed(buf.at[pl.ds(0, buf.shape[0] - 1)], red_send.at[stage])
    landed(slabs.at[pl.ds(0, 3)], send)
    landed(dens.at[pl.ds(0, 31 * 32)], out_send)
    landed(out, out_recv)


def body(record, last_slab):
    cells = float(record.shape[1] * record.shape[2] * lax.axis_size("space") * record.shape[3])
    dma = pltpu.SemaphoreType.DMA
    tiles, top = pl.pallas_call(
        functools.partial(kernel, cells),
        out_shape=(jax.ShapeDtypeStruct((1024, 128), F32), jax.ShapeDtypeStruct((1, 2), F32)),
        in_specs=[
            pl.BlockSpec(memory_space=pl.ANY),
            pl.BlockSpec(memory_space=pl.ANY),
        ],
        out_specs=(pl.BlockSpec(memory_space=pl.ANY), pl.BlockSpec(memory_space=pltpu.VMEM)),
        scratch_shapes=[
            pltpu.VMEM((5, 6, 32, 16, 128), BF16),
            pltpu.VMEM((512, 160), BF16),
            pltpu.VMEM((512, 128), F32),
            pltpu.VMEM((8, 160, 256), BF16),
            pltpu.VMEM((256, 256), F32),
            pltpu.VMEM((256, 256), F32),
            pltpu.VMEM((2, 16, 16, 32, 128), F32),
            pltpu.VMEM((512, 128), F32),
            pltpu.VMEM((128, 128), F32),
            pltpu.VMEM((4, 16, 8, 128), F32),
            pltpu.VMEM((1024, 128), F32),
            *[pltpu.VMEM((math.prod(SIZES[a] for a in axes), 4, 128), F32) for axes in GROUPS],
            dma(()),
            dma((6,)),
            dma((len(GROUPS),)),
            dma((len(GROUPS),)),
            dma(()),
            dma(()),
            pltpu.SemaphoreType.REGULAR((3,)),
        ],
        compiler_params=pltpu.CompilerParams(
            collective_id=0, has_side_effects=True, vmem_limit_bytes=52 << 20
        ),
        name="modes",
    )(record, last_slab)
    density = tiles.reshape(64, 2, 8, 128).transpose(0, 2, 1, 3).reshape(1, 512, 256)
    return density, top


def solution(mesh):
    return jax.shard_map(
        body,
        mesh=mesh,
        in_specs=(P("tm", None, "space", None), P(None, None, "space", None)),
        out_specs=(P("space", None, "tm"), P("space", None)),
        check_vma=False,
    )
```

```python
import functools
import math

import jax
import jax.numpy as jnp
import numpy as np
from jax import lax
from jax.experimental import pallas as pl
from jax.experimental.pallas import tpu as pltpu
from jax.sharding import PartitionSpec as P

SWEEPS = 5
MESH = pl.DeviceIdType.MESH
F32 = jnp.float32
BF16 = jnp.bfloat16
PAIRS = [(b, c) for b in range(4) for c in range(b + 1, 4)]
SIZES = {"y": 4, "z": 4, "x": 4, "c": 2}
ROUNDS = [((0, 1), (2, 3)), ((0, 2), (1, 3)), ((0, 3), (1, 2))]


def dft_rows():
    row = lax.broadcasted_iota(jnp.int32, (128, 96), 0)
    t = lax.broadcasted_iota(jnp.int32, (128, 96), 1) - 32 * ((row >> 5) & 1)
    turn = 2.0 * np.pi / 64.0
    taper = np.sqrt(8.0 / 3.0) / 16.0 * (1.0 - jnp.cos(turn * t.astype(F32)))
    phase = ((row & 31) * t + jnp.where(row >= 64, 16, 0) + 32) & 63
    wave = jnp.cos(turn * (phase - 32).astype(F32))
    return jnp.where((t >= 0) & (t < 64), taper * wave, 0.0)


def peers_along(axes, me):
    out = []
    offsets = [{}]
    for a in axes:
        offsets = [dict(o, **{a: d}) for o in offsets for d in range(SIZES[a])]
    for o in offsets:
        if any(o.values()):
            at = {a: (me[a] ^ o[a]) if o.get(a) else me[a] for a in me}
            out.append((at["y"], at["z"] * 8 + at["x"] * 2 + at["c"]))
    return out


def place(axes, me):
    index = 0
    for a in axes:
        index = index * SIZES[a] + me[a]
    return index


GROUPS = ("zxc", "y")


def eigen_modes(diag, off):
    zero = jnp.zeros_like(diag[0])
    copy = lax.broadcasted_iota(jnp.int32, zero.shape, 1) >> 5
    vecs = [(jnp.where(copy == k, 1.0, 0.0), zero) for k in range(4)]

    def sweep(_, state):
        diag, mat, vecs = list(state[0]), dict(zip(PAIRS, state[1])), list(state[2])

        def get(i, k):
            if i < k:
                return mat[(i, k)]
            re, im = mat[(k, i)]
            return re, -im

        def put(i, k, entry):
            mat[(min(i, k), max(i, k))] = entry if i < k else (entry[0], -entry[1])

        for pivots in ROUNDS:
            turns = []
            for p, q in pivots:
                g_re, g_im = mat[(p, q)]
                diff = diag[q] - diag[p]
                size = g_re * g_re + g_im * g_im
                gap = diff * diff + 4.0 * size
                some = gap > 0.0
                inverse = lax.rsqrt(jnp.where(some, gap, 1.0))
                square = jnp.where(some, 0.5 + 0.5 * jnp.abs(diff) * inverse, 1.0)
                secant = lax.rsqrt(square)
                signed = jnp.where(diff >= 0.0, inverse, -inverse)
                factor = signed * secant
                turns.append((p, q, square * secant, factor * g_re, -factor * g_im, size * factor * secant))
            for p, q, cosine, s_re, s_im, shift in turns:
                diag[p], diag[q] = diag[p] - shift, diag[q] + shift
                mat[(p, q)] = (zero, zero)

                def rotate(col_p, col_q):
                    (pr, pi), (qr, qi) = col_p, col_q
                    new_p = (cosine * pr - (s_re * qr - s_im * qi), cosine * pi - (s_re * qi + s_im * qr))
                    new_q = (cosine * qr + (s_re * pr + s_im * pi), cosine * qi + (s_re * pi - s_im * pr))
                    return new_p, new_q

                for i in range(4):
                    if i not in (p, q):
                        new_p, new_q = rotate(get(i, p), get(i, q))
                        put(i, p, new_p)
                        put(i, q, new_q)
                vecs[p], vecs[q] = rotate(vecs[p], vecs[q])
        return diag, [mat[pq] for pq in PAIRS], vecs

    state = (list(diag), [off[pq] for pq in PAIRS], vecs)
    diag, _, vecs = lax.fori_loop(0, SWEEPS, sweep, state)
    return diag, vecs


def mode_terms(total, cells):
    def spread(k):
        part = total[k // 4 : k // 4 + 1, 32 * (k % 4) : 32 * (k % 4) + 32] * (1.0 / cells)
        return jnp.concatenate([part] * 4, 1)

    sums = [spread(k) for k in range(16)]
    off = {pq: (sums[4 + i], sums[10 + i]) for i, pq in enumerate(PAIRS)}
    diag, vecs = eigen_modes(sums[:4], off)
    hi0, lo0 = jnp.maximum(diag[0], diag[1]), jnp.minimum(diag[0], diag[1])
    hi1, lo1 = jnp.maximum(diag[2], diag[3]), jnp.minimum(diag[2], diag[3])
    first = jnp.maximum(hi0, hi1)
    mid0, mid1 = jnp.minimum(hi0, hi1), jnp.maximum(lo0, lo1)
    second, third = jnp.maximum(mid0, mid1), jnp.minimum(mid0, mid1)
    norm = (first + 1e-06) * (first + 1e-06)
    lift = [jnp.maximum(d - third, 0.0) / norm for d in diag]
    mode = []
    for d in range(3):
        re, im = 0.0, 0.0
        for k in range(4):
            ar, ai = vecs[k]
            br, bi = (pltpu.roll(v, 128 - 32 * d, 1) if d else v for v in vecs[k])
            re = re + lift[k] * (ar * br + ai * bi)
            im = im + lift[k] * (ai * br - ar * bi)
        mode.append((re, im))
    terms = [mode[0][0][:, 32 * b : 32 * b + 32] for b in range(4)]
    for part in range(2):
        for b, c in PAIRS:
            d = c - b
            at, sign = (b, 1.0) if d < 3 else (3, (1.0, -1.0)[part])
            entry = mode[d if d < 3 else 1][part][:, 32 * at : 32 * at + 32]
            terms.append((2.0, -2.0)[part] * sign * entry)
    return terms, first[:, 0:32], second[:, 0:32]


def kernel(
    cells, record, last, out, top,
    slabs, split, wide0, wide1, series, spec, prods, sums, turned, weights, dens, *rest,
):
    tm, space = lax.axis_index("tm"), lax.axis_index("space")
    me = {"y": tm, "z": space >> 3, "x": (space >> 1) & 3, "c": space & 1}
    parts = rest[: len(GROUPS)]
    send, recv, red_send, red_recv, out_send, out_recv, meet = rest[len(GROUPS) :]

    near = [peer for axis in "cxzy" for peer in peers_along(axis, me)]

    def greet(semaphore):
        for peer in near:
            pl.semaphore_signal(semaphore, inc=1, device_id=peer, device_id_type=MESH)

    def landed(ref, semaphore):
        pltpu.make_async_copy(ref, ref, semaphore).wait()

    barrier = pltpu.get_barrier_semaphore()
    greet(barrier)

    def quarter(ref, piece, to):
        half, comp = piece // 3, piece % 3
        return ref.at[:, comp, :, pl.ds(pl.multiple_of(to * 256 + half * 128, 128), 128)]

    def slab_copy(piece, d):
        to = tm ^ d
        return pltpu.make_async_remote_copy(
            src_ref=quarter(record, piece, to),
            dst_ref=slabs.at[tm, piece],
            send_sem=send,
            recv_sem=recv.at[piece],
            device_id=(to, space),
            device_id_type=MESH,
        )

    def own_copy(piece, which):
        ref, slot = ((record, tm), (last, 4))[which]
        return pltpu.make_async_copy(quarter(ref, piece, tm), slabs.at[slot, piece], recv.at[piece])

    for piece in range(6):
        for which in range(2):
            own_copy(piece, which).start()
    pl.semaphore_wait(barrier, len(near))
    for piece in range(6):
        for d in (2, 1, 3):
            slab_copy(piece, d).start()
    for turn in range(3):
        greet(meet.at[turn])
        pl.semaphore_wait(meet.at[turn], len(near))

    zero = jnp.zeros((8, 128), F32)
    table = dft_rows()
    upper = table.astype(BF16)
    split[...] = jnp.concatenate([upper, (table - upper.astype(F32)).astype(BF16)], 1)

    def transform(n):
        for pair in range(2):
            three = series[n, 64 * pair : 64 * pair + 96, :]
            twice = jnp.concatenate([three, three], 0)
            spec[n, 128 * pair : 128 * pair + 128, :] = jnp.dot(split[...], twice, preferred_element_type=F32)

    def multiply(half, comp):
        for g in range(4):
            acc = [zero] * 16
            for n in range(8):
                for i in range(2):
                    x = [spec[n, 32 * m + 8 * g : 32 * m + 8 * g + 8, 128 * i : 128 * i + 128] for m in range(8)]
                    a, b = x[0:2] + x[4:6], x[2:4] + x[6:8]
                    terms = [a[u] * a[u] + b[u] * b[u] for u in range(4)]
                    terms += [a[u] * a[v] + b[u] * b[v] for u, v in PAIRS]
                    terms += [a[u] * b[v] - b[u] * a[v] for u, v in PAIRS]
                    for k in range(16):
                        if comp > 0:
                            terms[k] += prods[half, 2 * n + i, k, 8 * g : 8 * g + 8, :]
                        prods[half, 2 * n + i, k, 8 * g : 8 * g + 8, :] = terms[k]
                        acc[k] = acc[k] + terms[k]
            if comp == 2:
                for k in range(16):
                    at = slice(32 * k + 8 * g, 32 * k + 8 * g + 8)
                    sums[at, :] = acc[k] if half == 0 else sums[at, :] + acc[k]

    for piece in range(6):
        half, comp = divmod(piece, 3)
        landed(slabs.at[:, piece], recv.at[piece])
        for slab in range(5):
            wide = (wide0, wide1)[slab % 2]
            wide[...] = slabs[slab, piece].astype(F32).reshape(512, 128)
            for r in range(16):
                lines = wide[pl.ds(r, 32, stride=16), :].astype(BF16)
                series[r // 2, 32 * slab : 32 * slab + 32, 128 * (r % 2) : 128 * (r % 2) + 128] = lines
        for n in range(8):
            transform(n)
        multiply(half, comp)

    total = jnp.concatenate(
        [jnp.sum(jnp.transpose(sums[128 * i : 128 * i + 128, :]), axis=0, keepdims=True) for i in range(4)], 0
    )

    for stage, (axes, buf) in enumerate(zip(GROUPS, parts)):
        mine = place(axes, me)
        buf[mine] = total
        for peer in peers_along(axes, me):
            pltpu.make_async_remote_copy(
                src_ref=buf.at[mine],
                dst_ref=buf.at[mine],
                send_sem=red_send.at[stage],
                recv_sem=red_recv.at[stage],
                device_id=peer,
                device_id_type=MESH,
            ).start()
        landed(buf.at[pl.ds(0, buf.shape[0] - 1)], red_recv.at[stage])
        total = jnp.sum(buf[...], axis=0)

    terms, first, second = mode_terms(total, cells)
    here = lax.broadcasted_iota(jnp.int32, (1, 32), 1) == space
    pick = [jnp.sum(jnp.where(here, v, 0.0), axis=1, keepdims=True) for v in (first, second)]
    top[...] = jnp.concatenate(pick, 1)

    for k in range(16):
        turned[k : k + 1, 0:32] = terms[k]
    columns = jnp.transpose(turned[...])

    for g in range(4):
        for k in range(16):
            weights[g, k] = jnp.broadcast_to(columns[8 * g : 8 * g + 8, k : k + 1], (8, 128))

    def tiles_of(index):
        return pl.ds(pl.multiple_of(index * 32, 32), 32)

    kept = pltpu.make_async_copy(dens.at[tiles_of(space)], out.at[tiles_of(space)], out_recv)
    for step in range(4):
        g = me["z"] ^ step
        band = pl.ds(pl.multiple_of(8 * g, 8), 8)
        weight = [weights[g, k] for k in range(16)]

        def collect(r, _, g=g, band=band, weight=weight):
            for half in range(2):
                parts = [weight[k] * prods[half, r, k, band, :] for k in range(16)]
                while len(parts) > 1:
                    parts = [parts[k] + parts[k + 1] for k in range(0, len(parts), 2)]
                dens[pl.ds(256 * g + 16 * (r // 8) + 8 * half + r % 8, 8, stride=32), :] = parts[0]
            return 0

        lax.fori_loop(0, 16, collect, 0, unroll=4)
        for i in range(8):
            if step == 0 and i == 0:
                kept.start()
                continue
            d = 8 * step + i
            peer = space ^ d
            pltpu.make_async_remote_copy(
                src_ref=dens.at[tiles_of(peer)],
                dst_ref=out.at[tiles_of(space)],
                send_sem=out_send,
                recv_sem=out_recv,
                device_id=(tm, peer),
                device_id_type=MESH,
            ).start()
    for stage, buf in enumerate(parts):
        landed(buf.at[pl.ds(0, buf.shape[0] - 1)], red_send.at[stage])
    landed(slabs.at[pl.ds(0, 3)], send)
    landed(dens.at[pl.ds(0, 31 * 32)], out_send)
    landed(out, out_recv)


def body(record, last_slab):
    cells = float(record.shape[1] * record.shape[2] * lax.axis_size("space") * record.shape[3])
    dma = pltpu.SemaphoreType.DMA
    tiles, top = pl.pallas_call(
        functools.partial(kernel, cells),
        out_shape=(jax.ShapeDtypeStruct((1024, 128), F32), jax.ShapeDtypeStruct((1, 2), F32)),
        in_specs=[
            pl.BlockSpec(memory_space=pl.ANY),
            pl.BlockSpec(memory_space=pl.ANY),
        ],
        out_specs=(pl.BlockSpec(memory_space=pl.ANY), pl.BlockSpec(memory_space=pltpu.VMEM)),
        scratch_shapes=[
            pltpu.VMEM((5, 6, 32, 16, 128), BF16),
            pltpu.VMEM((128, 192), BF16),
            pltpu.VMEM((512, 128), F32),
            pltpu.VMEM((512, 128), F32),
            pltpu.VMEM((8, 160, 256), BF16),
            pltpu.VMEM((8, 256, 256), F32),
            pltpu.VMEM((2, 16, 16, 32, 128), F32),
            pltpu.VMEM((512, 128), F32),
            pltpu.VMEM((128, 128), F32),
            pltpu.VMEM((4, 16, 8, 128), F32),
            pltpu.VMEM((1024, 128), F32),
            *[pltpu.VMEM((math.prod(SIZES[a] for a in axes), 4, 128), F32) for axes in GROUPS],
            dma(()),
            dma((6,)),
            dma((len(GROUPS),)),
            dma((len(GROUPS),)),
            dma(()),
            dma(()),
            pltpu.SemaphoreType.REGULAR((3,)),
        ],
        compiler_params=pltpu.CompilerParams(
            collective_id=0, has_side_effects=True, vmem_limit_bytes=52 << 20
        ),
        name="modes",
    )(record, last_slab)
    density = tiles.reshape(64, 2, 8, 128).transpose(0, 2, 1, 3).reshape(1, 512, 256)
    return density, top


def solution(mesh):
    return jax.shard_map(
        body,
        mesh=mesh,
        in_specs=(P("tm", None, "space", None), P(None, None, "space", None)),
        out_specs=(P("space", None, "tm"), P("space", None)),
        check_vma=False,
    )
```

```python
import functools
import math

import jax
import jax.numpy as jnp
import numpy as np
from jax import lax
from jax.experimental import pallas as pl
from jax.experimental.pallas import tpu as pltpu
from jax.sharding import PartitionSpec as P

SWEEPS = 5
MESH = pl.DeviceIdType.MESH
F32 = jnp.float32
BF16 = jnp.bfloat16
PAIRS = [(b, c) for b in range(4) for c in range(b + 1, 4)]
SIZES = {"y": 4, "z": 4, "x": 4, "c": 2}
ROUNDS = [((0, 1), (2, 3)), ((0, 2), (1, 3)), ((0, 3), (1, 2))]


def dft_rows():
    row = lax.broadcasted_iota(jnp.int32, (128, 96), 0)
    t = lax.broadcasted_iota(jnp.int32, (128, 96), 1) - 32 * ((row >> 5) & 1)
    turn = 2.0 * np.pi / 64.0
    taper = np.sqrt(8.0 / 3.0) / 16.0 * (1.0 - jnp.cos(turn * t.astype(F32)))
    phase = ((row & 31) * t + jnp.where(row >= 64, 16, 0) + 32) & 63
    wave = jnp.cos(turn * (phase - 32).astype(F32))
    return jnp.where((t >= 0) & (t < 64), taper * wave, 0.0)


def peers_along(axes, me):
    out = []
    offsets = [{}]
    for a in axes:
        offsets = [dict(o, **{a: d}) for o in offsets for d in range(SIZES[a])]
    for o in offsets:
        if any(o.values()):
            at = {a: (me[a] ^ o[a]) if o.get(a) else me[a] for a in me}
            out.append((at["y"], at["z"] * 8 + at["x"] * 2 + at["c"]))
    return out


def place(axes, me):
    index = 0
    for a in axes:
        index = index * SIZES[a] + me[a]
    return index


GROUPS = ("zxc", "y")


def eigen_modes(diag, off):
    zero = jnp.zeros_like(diag[0])
    copy = lax.broadcasted_iota(jnp.int32, zero.shape, 1) >> 5
    vecs = [(jnp.where(copy == k, 1.0, 0.0), zero) for k in range(4)]

    def sweep(_, state):
        diag, mat, vecs = list(state[0]), dict(zip(PAIRS, state[1])), list(state[2])

        def get(i, k):
            if i < k:
                return mat[(i, k)]
            re, im = mat[(k, i)]
            return re, -im

        def put(i, k, entry):
            mat[(min(i, k), max(i, k))] = entry if i < k else (entry[0], -entry[1])

        for pivots in ROUNDS:
            turns = []
            for p, q in pivots:
                g_re, g_im = mat[(p, q)]
                diff = diag[q] - diag[p]
                size = g_re * g_re + g_im * g_im
                gap = diff * diff + 4.0 * size
                some = gap > 0.0
                inverse = lax.rsqrt(jnp.where(some, gap, 1.0))
                square = jnp.where(some, 0.5 + 0.5 * jnp.abs(diff) * inverse, 1.0)
                secant = lax.rsqrt(square)
                signed = jnp.where(diff >= 0.0, inverse, -inverse)
                factor = signed * secant
                turns.append((p, q, square * secant, factor * g_re, -factor * g_im, size * factor * secant))
            for p, q, cosine, s_re, s_im, shift in turns:
                diag[p], diag[q] = diag[p] - shift, diag[q] + shift
                mat[(p, q)] = (zero, zero)

                def rotate(col_p, col_q):
                    (pr, pi), (qr, qi) = col_p, col_q
                    new_p = (cosine * pr - (s_re * qr - s_im * qi), cosine * pi - (s_re * qi + s_im * qr))
                    new_q = (cosine * qr + (s_re * pr + s_im * pi), cosine * qi + (s_re * pi - s_im * pr))
                    return new_p, new_q

                for i in range(4):
                    if i not in (p, q):
                        new_p, new_q = rotate(get(i, p), get(i, q))
                        put(i, p, new_p)
                        put(i, q, new_q)
                vecs[p], vecs[q] = rotate(vecs[p], vecs[q])
        return diag, [mat[pq] for pq in PAIRS], vecs

    state = (list(diag), [off[pq] for pq in PAIRS], vecs)
    diag, _, vecs = lax.fori_loop(0, SWEEPS, sweep, state)
    return diag, vecs


def mode_terms(total, cells):
    def spread(k):
        part = total[k // 4 : k // 4 + 1, 32 * (k % 4) : 32 * (k % 4) + 32] * (1.0 / cells)
        return jnp.concatenate([part] * 4, 1)

    sums = [spread(k) for k in range(16)]
    off = {pq: (sums[4 + i], sums[10 + i]) for i, pq in enumerate(PAIRS)}
    diag, vecs = eigen_modes(sums[:4], off)
    hi0, lo0 = jnp.maximum(diag[0], diag[1]), jnp.minimum(diag[0], diag[1])
    hi1, lo1 = jnp.maximum(diag[2], diag[3]), jnp.minimum(diag[2], diag[3])
    first = jnp.maximum(hi0, hi1)
    mid0, mid1 = jnp.minimum(hi0, hi1), jnp.maximum(lo0, lo1)
    second, third = jnp.maximum(mid0, mid1), jnp.minimum(mid0, mid1)
    norm = (first + 1e-06) * (first + 1e-06)
    lift = [jnp.maximum(d - third, 0.0) / norm for d in diag]
    mode = []
    for d in range(3):
        re, im = 0.0, 0.0
        for k in range(4):
            ar, ai = vecs[k]
            br, bi = (pltpu.roll(v, 128 - 32 * d, 1) if d else v for v in vecs[k])
            re = re + lift[k] * (ar * br + ai * bi)
            im = im + lift[k] * (ai * br - ar * bi)
        mode.append((re, im))
    terms = [mode[0][0][:, 32 * b : 32 * b + 32] for b in range(4)]
    for part in range(2):
        for b, c in PAIRS:
            d = c - b
            at, sign = (b, 1.0) if d < 3 else (3, (1.0, -1.0)[part])
            entry = mode[d if d < 3 else 1][part][:, 32 * at : 32 * at + 32]
            terms.append((2.0, -2.0)[part] * sign * entry)
    return terms, first[:, 0:32], second[:, 0:32]


def kernel(
    cells, record, last, out, top,
    slabs, split, wide0, wide1, series, spec, prods, sums, turned, weights, dens, *rest,
):
    tm, space = lax.axis_index("tm"), lax.axis_index("space")
    me = {"y": tm, "z": space >> 3, "x": (space >> 1) & 3, "c": space & 1}
    parts = rest[: len(GROUPS)]
    send, recv, red_send, red_recv, out_send, out_recv, meet = rest[len(GROUPS) :]

    near = [peer for axis in "cxzy" for peer in peers_along(axis, me)]

    def greet(semaphore):
        for peer in near:
            pl.semaphore_signal(semaphore, inc=1, device_id=peer, device_id_type=MESH)

    def landed(ref, semaphore):
        pltpu.make_async_copy(ref, ref, semaphore).wait()

    barrier = pltpu.get_barrier_semaphore()
    greet(barrier)

    def quarter(ref, piece, to):
        half, comp = piece // 3, piece % 3
        return ref.at[:, comp, :, pl.ds(pl.multiple_of(to * 256 + half * 128, 128), 128)]

    def slab_copy(piece, d):
        to = tm ^ d
        return pltpu.make_async_remote_copy(
            src_ref=quarter(record, piece, to),
            dst_ref=slabs.at[tm, piece],
            send_sem=send,
            recv_sem=recv.at[piece],
            device_id=(to, space),
            device_id_type=MESH,
        )

    def own_copy(piece, which):
        ref, slot = ((record, tm), (last, 4))[which]
        return pltpu.make_async_copy(quarter(ref, piece, tm), slabs.at[slot, piece], recv.at[piece])

    for piece in range(6):
        for which in range(2):
            own_copy(piece, which).start()
    pl.semaphore_wait(barrier, len(near))
    for piece in range(6):
        for d in (2, 1, 3):
            slab_copy(piece, d).start()
    for turn in range(3):
        greet(meet.at[turn])
        pl.semaphore_wait(meet.at[turn], len(near))

    zero = jnp.zeros((8, 128), F32)
    table = dft_rows()
    upper = table.astype(BF16)
    split[...] = jnp.concatenate([upper, (table - upper.astype(F32)).astype(BF16)], 1)

    def transform(n):
        for pair in range(2):
            three = series[n, 64 * pair : 64 * pair + 96, :]
            twice = jnp.concatenate([three, three], 0)
            spec[n, 128 * pair : 128 * pair + 128, :] = jnp.dot(split[...], twice, preferred_element_type=F32)

    def multiply(half, comp):
        for g in range(4):
            acc = [zero] * 16
            for n in range(8):
                for i in range(2):
                    x = [spec[n, 32 * m + 8 * g : 32 * m + 8 * g + 8, 128 * i : 128 * i + 128] for m in range(8)]
                    a, b = x[0:2] + x[4:6], x[2:4] + x[6:8]
                    terms = [a[u] * a[u] + b[u] * b[u] for u in range(4)]
                    terms += [a[u] * a[v] + b[u] * b[v] for u, v in PAIRS]
                    terms += [a[u] * b[v] - b[u] * a[v] for u, v in PAIRS]
                    for k in range(16):
                        if comp > 0:
                            terms[k] += prods[half, 2 * n + i, k, 8 * g : 8 * g + 8, :]
                        prods[half, 2 * n + i, k, 8 * g : 8 * g + 8, :] = terms[k]
                        acc[k] = acc[k] + terms[k]
            if comp == 2:
                for k in range(16):
                    at = slice(32 * k + 8 * g, 32 * k + 8 * g + 8)
                    sums[at, :] = acc[k] if half == 0 else sums[at, :] + acc[k]

    for piece in range(6):
        half, comp = divmod(piece, 3)
        landed(slabs.at[:, piece], recv.at[piece])
        for slab in range(5):
            wide = (wide0, wide1)[slab % 2]
            wide[...] = slabs[slab, piece].astype(F32).reshape(512, 128)
            for r in range(16):
                lines = wide[pl.ds(r, 32, stride=16), :].astype(BF16)
                series[r // 2, 32 * slab : 32 * slab + 32, 128 * (r % 2) : 128 * (r % 2) + 128] = lines
        for n in range(8):
            transform(n)
        multiply(half, comp)

    total = jnp.concatenate(
        [jnp.sum(jnp.transpose(sums[128 * i : 128 * i + 128, :]), axis=0, keepdims=True) for i in range(4)], 0
    )

    for stage, (axes, buf) in enumerate(zip(GROUPS, parts)):
        mine = place(axes, me)
        buf[mine] = total
        for peer in peers_along(axes, me):
            pltpu.make_async_remote_copy(
                src_ref=buf.at[mine],
                dst_ref=buf.at[mine],
                send_sem=red_send.at[stage],
                recv_sem=red_recv.at[stage],
                device_id=peer,
                device_id_type=MESH,
            ).start()
        landed(buf.at[pl.ds(0, buf.shape[0] - 1)], red_recv.at[stage])
        total = jnp.sum(buf[...], axis=0)

    terms, first, second = mode_terms(total, cells)
    for k in range(16):
        turned[k : k + 1, 0:32] = terms[k]
    columns = jnp.transpose(turned[...])

    for g in range(4):
        for k in range(16):
            weights[g, k] = jnp.broadcast_to(columns[8 * g : 8 * g + 8, k : k + 1], (8, 128))

    def tiles_of(index):
        return pl.ds(pl.multiple_of(index * 32, 32), 32)

    kept = pltpu.make_async_copy(dens.at[tiles_of(space)], out.at[tiles_of(space)], out_recv)
    for step in range(4):
        g = me["z"] ^ step
        band = pl.ds(pl.multiple_of(8 * g, 8), 8)

        def collect(r, _, g=g, band=band):
            for half in range(2):
                terms = [weights[g, k] * prods[half, r, k, band, :] for k in range(16)]
                while len(terms) > 1:
                    terms = [terms[k] + terms[k + 1] for k in range(0, len(terms), 2)]
                dens[pl.ds(256 * g + 16 * (r // 8) + 8 * half + r % 8, 8, stride=32), :] = terms[0]
            return 0

        lax.fori_loop(0, 16, collect, 0, unroll=4)
        for i in range(8):
            if step == 0 and i == 0:
                kept.start()
                continue
            d = 8 * step + i
            peer = space ^ d
            pltpu.make_async_remote_copy(
                src_ref=dens.at[tiles_of(peer)],
                dst_ref=out.at[tiles_of(space)],
                send_sem=out_send,
                recv_sem=out_recv,
                device_id=(tm, peer),
                device_id_type=MESH,
            ).start()
    here = lax.broadcasted_iota(jnp.int32, (1, 32), 1) == space
    pick = [jnp.sum(jnp.where(here, v, 0.0), axis=1, keepdims=True) for v in (first, second)]
    top[...] = jnp.concatenate(pick, 1)
    for stage, buf in enumerate(parts):
        landed(buf.at[pl.ds(0, buf.shape[0] - 1)], red_send.at[stage])
    landed(slabs.at[pl.ds(0, 3)], send)
    landed(dens.at[pl.ds(0, 31 * 32)], out_send)
    landed(out, out_recv)


def body(record, last_slab):
    cells = float(record.shape[1] * record.shape[2] * lax.axis_size("space") * record.shape[3])
    dma = pltpu.SemaphoreType.DMA
    tiles, top = pl.pallas_call(
        functools.partial(kernel, cells),
        out_shape=(jax.ShapeDtypeStruct((1024, 128), F32), jax.ShapeDtypeStruct((1, 2), F32)),
        in_specs=[
            pl.BlockSpec(memory_space=pl.ANY),
            pl.BlockSpec(memory_space=pl.ANY),
        ],
        out_specs=(pl.BlockSpec(memory_space=pl.ANY), pl.BlockSpec(memory_space=pltpu.VMEM)),
        scratch_shapes=[
            pltpu.VMEM((5, 6, 32, 16, 128), BF16),
            pltpu.VMEM((128, 192), BF16),
            pltpu.VMEM((512, 128), F32),
            pltpu.VMEM((512, 128), F32),
            pltpu.VMEM((8, 160, 256), BF16),
            pltpu.VMEM((8, 256, 256), F32),
            pltpu.VMEM((2, 16, 16, 32, 128), F32),
            pltpu.VMEM((512, 128), F32),
            pltpu.VMEM((128, 128), F32),
            pltpu.VMEM((4, 16, 8, 128), F32),
            pltpu.VMEM((1024, 128), F32),
            *[pltpu.VMEM((math.prod(SIZES[a] for a in axes), 4, 128), F32) for axes in GROUPS],
            dma(()),
            dma((6,)),
            dma((len(GROUPS),)),
            dma((len(GROUPS),)),
            dma(()),
            dma(()),
            pltpu.SemaphoreType.REGULAR((3,)),
        ],
        compiler_params=pltpu.CompilerParams(
            collective_id=0, has_side_effects=True, vmem_limit_bytes=52 << 20
        ),
        name="modes",
    )(record, last_slab)
    density = tiles.reshape(64, 2, 8, 128).transpose(0, 2, 1, 3).reshape(1, 512, 256)
    return density, top


def solution(mesh):
    return jax.shard_map(
        body,
        mesh=mesh,
        in_specs=(P("tm", None, "space", None), P(None, None, "space", None)),
        out_specs=(P("space", None, "tm"), P("space", None)),
        check_vma=False,
    )
```
